32 devices in a mesh: blk: 32 (over z, y, x, core).
Axes of the slice: x: 2, y: 2, z: 4, core: 2. Of those that a mesh axis runs over, the one named last changes fastest.
Arguments:
- points: bfloat16 [32768, 128], P('blk'), may hold values from -6 to 6
- targets: float32 [32768, 64], P('blk'), may hold values from -6 to 6
- masks: int32 [2], replicated, may hold values from 1 to 31, as said below
Outputs:
- solution: float32 [32768, 64], P('blk')
- residual: float32 [32768, 64], P('blk')
The draws below stay inside these ranges and needn't reach their ends.
Inputs may be any that keep to these rules, and one draw needn't show every extreme that they name: `masks`: the 2 values are distinct, and one of them is 31.
All inputs are finite; a program needn't handle non-finite values.
Results may differ from the reference program's by a relative error of at most 0.00057.
Values may be sent and summed in bfloat16 or wider, within the bound.
No kernel may reach another device: no remote copies, remote signals or barrier semaphores. Data moves between devices by JAX's collectives and lax.ppermute only.
A program may use at most 64 MiB of HBM per device.

```python
import jax
import jax.numpy as jnp
from jax import lax

PTS_DEV = 1024
FEAT = 128
RHS = 64
ROUNDS = 2
ITERS = 2
POINTS = 32768
N_BLK = 32


def draw_masks(key, part):
    key = jax.random.fold_in(key, 7)
    first, second = jax.random.split(key)
    others = jax.random.permutation(first, N_BLK - 2)[:ROUNDS - 1] + 1
    values = jnp.concatenate([jnp.full((1,), N_BLK - 1, jnp.int32), others.astype(jnp.int32)])
    return jax.random.permutation(second, values).astype(jnp.int32)


def draw_points(key, part):
    key = jax.random.fold_in(key, 11)
    first = jax.random.fold_in(key, 0)
    second = jax.random.fold_in(key, 1)
    fourth = jax.random.fold_in(key, 3)
    signs = jnp.where(jax.random.bernoulli(second, 0.5, (FEAT,)), 1.0, -1.0).astype(jnp.float32)
    latent = jax.random.uniform(first, (POINTS, 4), jnp.float32, -2.0, 2.0)
    gains = 2.0 * signs
    noise = 0.3 * jnp.clip(jax.random.normal(fourth, (POINTS, FEAT), jnp.float32), -3.0, 3.0)
    spread = jnp.tile(latent, (1, FEAT // 4))
    values = spread * gains[None, :] + noise
    return values.astype(jnp.bfloat16)


def level_of(stream_key, dims, shards, smallest, high):
    gain, own = 1.0, jax.random.fold_in(stream_key, 6)
    for dim, parts in shards:
        steps = jnp.exp(jax.random.uniform(jax.random.fold_in(own, dim), (parts,), jnp.float32, smallest / len(shards), high / len(shards)))
        gain = gain * jnp.repeat(steps, dims[dim] // parts).reshape([-1 if axis == dim else 1 for axis in range(len(dims))])
    return gain


def gaussian(own_key, extent, scale, bound, shards=(), kind=jnp.bfloat16):
    drawn = jax.random.normal(own_key, extent, jnp.float32) * scale
    if len(shards) > 0:
        drawn = level_of(own_key, extent, shards, -0.22, 0.18) * drawn
    return jnp.clip(drawn, min=-bound, max=bound).astype(kind)


def setup_inputs(seed: int = 0) -> dict:
    streams_of = jax.random.split(jax.random.key(seed), 4)
    points = draw_points(jax.random.fold_in(streams_of[3], 71), 0)
    targets = gaussian(streams_of[1], (POINTS, RHS), 1.0, 6.0, ((0, 32),), jnp.float32)
    masks = draw_masks(jax.random.fold_in(streams_of[3], 71), 0)
    return dict(points=points, targets=targets, masks=masks)


def kernel_tile(left, right):
    left_sq = jnp.sum(jnp.square(left.astype(jnp.float32)), axis=1)
    right_sq = jnp.sum(jnp.square(right.astype(jnp.float32)), axis=1)
    inner = jnp.dot(left, right.T, preferred_element_type=jnp.float32)
    dist = left_sq[:, None] + right_sq[None, :] - 2.0 * inner
    return jnp.exp(-dist / FEAT).astype(jnp.bfloat16)


def operate(blocks, vector, masks):
    kernel_weight = 384.0 / ((ROUNDS + 1) * PTS_DEV)
    rounded = vector.astype(jnp.bfloat16).reshape(N_BLK, PTS_DEV, RHS)

    def one_block(index):
        own = blocks[index]
        total = jnp.dot(kernel_tile(own, own), rounded[index], preferred_element_type=jnp.float32)
        for turn in range(ROUNDS):
            other = jnp.bitwise_xor(index, masks[turn]).astype(jnp.int32)
            total = total + jnp.dot(kernel_tile(own, blocks[other]), rounded[other], preferred_element_type=jnp.float32)
        return total

    summed = lax.map(one_block, jnp.arange(N_BLK, dtype=jnp.int32)).reshape(POINTS, RHS)
    return 1.0 * vector + kernel_weight * summed


def reference(points, targets, masks):
    blocks = points.reshape(N_BLK, PTS_DEV, FEAT)
    lowest = 1.0
    highest = 25.0
    center = (highest + lowest) / 2.0
    half_span = (highest - lowest) / 2.0
    sigma_ratio = center / half_span
    ratio = 1.0 / sigma_ratio
    solution = jnp.zeros_like(targets)
    residual = targets
    direction = residual / center
    for count in range(ITERS):
        solution = solution + direction
        residual = residual - operate(blocks, direction, masks)
        following = 1.0 / (2.0 * sigma_ratio - ratio)
        direction = (following * ratio) * direction + (2.0 * following / half_span) * residual
        ratio = following
    return solution, residual
```

```python
import functools

import jax
import jax.numpy as jnp
from jax import lax
from jax.experimental import pallas as pl
from jax.experimental.pallas import tpu as pltpu
from jax.sharding import PartitionSpec as P

ROUNDS = 2
F32 = jnp.float32
BF16 = jnp.bfloat16
LOG2E = 1.4426950408889634
NN = (((1,), (0,)), ((), ()))
NT = (((1,), (1,)), ((), ()))
LOWEST, HIGHEST = 1.0, 25.0
CENTER = (HIGHEST + LOWEST) / 2.0
HALF = (HIGHEST - LOWEST) / 2.0
SIGMA = CENTER / HALF
FIRST = 1.0 / (2.0 * SIGMA - 1.0 / SIGMA)
KEEP = FIRST / SIGMA
GAIN = 2.0 * FIRST / HALF
ROWS = 256
PREP = 56
SHARES = (4,4)
PIECES = len(SHARES)


def dot(a, b, dims):
    return lax.dot_general(a, b, dims, preferred_element_type=F32)


def sides(x, left_ref, right_ref):
    feat = x.shape[1]
    xf = x.astype(F32)
    norm = jnp.sum(xf * xf, axis=1, keepdims=True) * (-1.0 / feat)
    high = norm.astype(BF16).astype(F32)
    mid = (norm - high).astype(BF16).astype(F32)
    low = norm - high - mid
    lane = lax.broadcasted_iota(jnp.int32, x.shape, 1)

    def extra(norms, ones):
        values = jnp.where((lane >= ones) & (lane < ones + 3), 1.0, 0.0)
        for place, part in enumerate((high, mid, low)):
            values = jnp.where(lane == norms + place, part, values)
        return values.astype(BF16)

    left_ref[:, :feat] = (xf * (2.0 / feat)).astype(BF16)
    left_ref[:, feat:] = extra(0, 3)
    if right_ref is not None:
        right_ref[:, :feat] = x
        right_ref[:, feat:] = extra(3, 0)


def tile_into(out, left, right):
    for at in range(0, left.shape[0], ROWS):
        out[at : at + ROWS, :] = jnp.exp2(dot(left[at : at + ROWS, :], right[...], NT) * LOG2E).astype(BF16)


def doubled(d):
    return jnp.concatenate([d, d], axis=0)


def forward(d, tile):
    return dot(doubled(d), tile, NN)[: d.shape[0]]


def across(d, tile):
    return dot(doubled(doubled(d)), tile, NT)[: d.shape[0]]


def following(targets, d, w):
    residual = targets - (d + w)
    return residual, KEEP * d + GAIN * residual


def spans(n):
    cuts = [n * sum(SHARES[:j]) // sum(SHARES) for j in range(PIECES + 1)]
    return [(a, b - a) for a, b in zip(cuts, cuts[1:])]


def prep_kernel(size, masks, x, t, whole, *rest):
    parts, branch, case, t_in, flags_in, sems = rest[:PIECES], *rest[PIECES:]
    n = x.shape[0]
    rhs = t.shape[0]
    flags = pltpu.make_async_copy(masks, flags_in, sems.at[2 + PIECES])
    flags.start()
    copies = [pltpu.make_async_copy(t, t_in, sems.at[0])]
    copies.append(pltpu.make_async_copy(x, whole.at[pl.ds(0, n)], sems.at[1]))
    for j, (at, rows) in enumerate(spans(n)):
        copies.append(
            pltpu.make_async_copy(x.at[pl.ds(at, rows)], parts[j].at[pl.ds(0, rows)], sems.at[2 + j])
        )
    for copy in copies:
        copy.start()
    flags.wait()
    first, second = flags_in[0], flags_in[1]
    other = jnp.where(first == size - 1, second, first)
    far = other >= size // 2
    case[0] = jnp.where(far, 1, 0)
    branch[0] = jnp.where(far, size - 1 - other, other) - 1
    copies[0].wait()
    d = (t_in[...] / CENTER).astype(BF16)
    for part, (at, rows) in zip((whole,) + tuple(parts), [(0, n)] + spans(n)):
        for j in range(rows // 128):
            part[rows + rhs * j : rows + rhs * (j + 1), :] = d[:, at + 128 * j : at + 128 * (j + 1)]
    for copy in copies[1:]:
        copy.wait()


def main_kernel(weight, case, x, t, near, *rest):
    far, late = rest[:PIECES], rest[PIECES : 2 * PIECES]
    (sol, res, xs, slabs, t_in, d_all, left, right, kept, once, sol_out, res_out, sems, more) = rest[2 * PIECES :]
    n, feat = x.shape
    rhs = t.shape[0]
    own = [
        pltpu.make_async_copy(x, xs.at[0], more.at[0]),
        pltpu.make_async_copy(t, t_in, more.at[1]),
    ]
    others = []
    for j, (start, rows) in enumerate(spans(n)):
        deep = rows * rhs // feat
        at, low = pl.ds(start, rows), pl.ds(start * rhs // feat, deep)
        for slot in (1, 2, 3):
            if slot == 1:
                sources = near.at[at], near.at[pl.ds(n + start * rhs // feat, deep)]
            else:
                packet = (far, late)[slot - 2][j]
                sources = packet.at[pl.ds(0, rows)], packet.at[pl.ds(rows, deep)]
            others.append(pltpu.make_async_copy(sources[0], xs.at[slot, at], sems.at[slot - 1, j]))
            others.append(pltpu.make_async_copy(sources[1], slabs.at[slot - 1, low], sems.at[slot - 1, PIECES + j]))
    for copy in own + others:
        copy.start()
    e, o = 1 + case[0], 2 - case[0]
    own[0].wait()
    sides(xs[0], left.at[0], right.at[0])
    tile_into(kept.at[0], left.at[0], right.at[0])
    own[1].wait()
    first = t_in[...] / CENTER
    d0 = first.astype(BF16)
    w0 = forward(d0, kept[0])
    for copy in others:
        copy.wait()
    for slot, source in ((1, e), (2, o), (3, 3)):
        for j in range(n // feat):
            d_all[slot - 1, :, feat * j : feat * (j + 1)] = slabs[source - 1, rhs * j : rhs * (j + 1), :]
        sides(xs[source], left.at[slot], None if slot == 2 else right.at[1 if slot == 1 else 2])
    de, do, da = d_all[0], d_all[1], d_all[2]
    tile_into(kept.at[1], left.at[1], right.at[0])
    tile_into(kept.at[2], left.at[3], right.at[0])
    tile_into(once.at[0], left.at[1], right.at[1])
    tile_into(once.at[1], left.at[2], right.at[1])
    tile_into(once.at[2], left.at[3], right.at[2])
    tile_into(once.at[3], left.at[2], right.at[2])
    w0 = w0 + forward(de, kept[1]) + forward(da, kept[2])
    we = across(d0, kept[1]) + forward(de, once[0]) + forward(do, once[1])
    wa = across(d0, kept[2]) + forward(da, once[2]) + forward(do, once[3])
    residual, second = following(t_in[...], first, weight * w0)
    e_first, a_first = de.astype(F32), da.astype(F32)
    _, e_second = following(e_first * CENTER, e_first, weight * we)
    _, a_second = following(a_first * CENTER, a_first, weight * wa)
    sol_out[...] = first + second
    sent = pltpu.make_async_copy(sol_out, sol, more.at[2])
    sent.start()
    w = forward(second.astype(BF16), kept[0])
    w = w + forward(e_second.astype(BF16), kept[1])
    w = w + forward(a_second.astype(BF16), kept[2])
    res_out[...] = residual - (second + weight * w)
    last = pltpu.make_async_copy(res_out, res, more.at[3])
    last.start()
    sent.wait()
    last.wait()


def call(kernel, outs, spaces, scratch, args, scalars, limit):
    hbm = pl.BlockSpec(memory_space=pl.ANY)
    smem = pl.BlockSpec(memory_space=pltpu.SMEM)
    return pl.pallas_call(
        kernel,
        out_shape=outs,
        in_specs=[smem] * scalars + [hbm] * (len(args) - scalars),
        out_specs=[pl.BlockSpec(memory_space=space) for space in spaces],
        scratch_shapes=scratch,
        compiler_params=pltpu.CompilerParams(vmem_limit_bytes=limit),
    )(*args)


def swap(array, mask):
    return lax.ppermute(array, "blk", [(i, i ^ mask) for i in range(lax.axis_size("blk"))])


def relay(array, mask):
    for bit in range(lax.axis_size("blk").bit_length() - 1):
        taken = jnp.bitwise_and(jnp.right_shift(mask, bit), 1) == 1
        array = jnp.where(taken, swap(array, 1 << bit), array)
    return array


def body(points, targets, masks):
    n, feat = points.shape
    rhs = targets.shape[1]
    size = lax.axis_size("blk")
    weight = 384.0 / ((ROUNDS + 1) * n)
    t = targets.T
    length = n + n * rhs // feat
    shape = jax.ShapeDtypeStruct
    dma = pltpu.SemaphoreType.DMA
    whole, *rest = call(
        functools.partial(prep_kernel, size),
        [shape((length, feat), BF16)]
        + [shape((rows * length // n, feat), BF16) for _, rows in spans(n)]
        + [shape((1,), jnp.int32)] * 2,
        [pltpu.VMEM] * (1 + PIECES) + [pltpu.SMEM] * 2,
        [pltpu.VMEM((rhs, n), F32), pltpu.SMEM((ROUNDS,), jnp.int32), dma((3 + PIECES,))],
        (masks, points, t),
        0,
        PREP << 20,
    )
    parts, branch, case = rest[:PIECES], rest[PIECES], rest[PIECES + 1]

    def exchange(mask):
        def run(whole, *parts):
            near = swap(whole, mask)
            across, beyond = [], []
            last = near
            for j, part in enumerate(parts):
                direct = swap(part, (size - 1) ^ mask if j % 2 == 0 else size - 1)
                direct, last = lax.optimization_barrier((direct, last))
                passed = swap(direct, mask)
                if j == 0:
                    near = last
                else:
                    beyond[-1] = last
                last = passed
                across.append(direct)
                beyond.append(passed)
            far = [(across, beyond)[j % 2][j] for j in range(PIECES)]
            late = [(beyond, across)[j % 2][j] for j in range(PIECES)]
            return near, far, late

        return run

    if size <= 32:
        near, far, late = lax.switch(
            branch[0], [exchange(mask) for mask in range(1, size // 2)], whole, *parts
        )
    else:
        mask = branch[0] + 1
        far = [relay(part, (size - 1) ^ mask) for part in parts]
        near, late = relay(whole, mask), [relay(part, mask) for part in far]
    sol, res = call(
        functools.partial(main_kernel, weight),
        [shape((rhs, n), F32)] * 2,
        [pl.ANY] * 2,
        [
            pltpu.VMEM((4, n, feat), BF16),
            pltpu.VMEM((3, n * rhs // feat, feat), BF16),
            pltpu.VMEM((rhs, n), F32),
            pltpu.VMEM((3, rhs, n), BF16),
            pltpu.VMEM((4, n, 2 * feat), BF16),
            pltpu.VMEM((3, n, 2 * feat), BF16),
            pltpu.VMEM((3, n, n), BF16),
            pltpu.VMEM((4, n, n), BF16),
            pltpu.VMEM((rhs, n), F32),
            pltpu.VMEM((rhs, n), F32),
            dma((3, 2 * PIECES)),
            dma((4,)),
        ],
        (case, points, t, near, *far, *late),
        1,
        40 << 20,
    )
    return sol.T, res.T


def solution(mesh):
    placed = (P("blk", None), P("blk", None), P())
    return jax.shard_map(
        body,
        mesh=mesh,
        in_specs=placed,
        out_specs=(P("blk", None), P("blk", None)),
        check_vma=False,
    )
```

```python
import functools

import jax
import jax.numpy as jnp
from jax import lax
from jax.experimental import pallas as pl
from jax.experimental.pallas import tpu as pltpu
from jax.sharding import PartitionSpec as P

ROUNDS = 2
F32 = jnp.float32
BF16 = jnp.bfloat16
LOG2E = 1.4426950408889634
NN = (((1,), (0,)), ((), ()))
NT = (((1,), (1,)), ((), ()))
LOWEST, HIGHEST = 1.0, 25.0
CENTER = (HIGHEST + LOWEST) / 2.0
HALF = (HIGHEST - LOWEST) / 2.0
SIGMA = CENTER / HALF
FIRST = 1.0 / (2.0 * SIGMA - 1.0 / SIGMA)
KEEP = FIRST / SIGMA
GAIN = 2.0 * FIRST / HALF
ROWS = 256
PREP = 56
SHARES = (4, 4)
PIECES = len(SHARES)


def dot(a, b, dims):
    return lax.dot_general(a, b, dims, preferred_element_type=F32)


def sides(x, left_ref, right_ref):
    feat = x.shape[1]
    xf = x.astype(F32)
    norm = jnp.sum(xf * xf, axis=1, keepdims=True) * (-1.0 / feat)
    high = norm.astype(BF16).astype(F32)
    mid = (norm - high).astype(BF16).astype(F32)
    low = norm - high - mid
    lane = lax.broadcasted_iota(jnp.int32, x.shape, 1)

    def extra(norms, ones):
        values = jnp.where((lane >= ones) & (lane < ones + 3), 1.0, 0.0)
        for place, part in enumerate((high, mid, low)):
            values = jnp.where(lane == norms + place, part, values)
        return values.astype(BF16)

    left_ref[:, :feat] = (xf * (2.0 / feat)).astype(BF16)
    left_ref[:, feat:] = extra(0, 3)
    if right_ref is not None:
        right_ref[:, :feat] = x
        right_ref[:, feat:] = extra(3, 0)


def tile_into(out, left, right):
    for at in range(0, left.shape[0], ROWS):
        out[at : at + ROWS, :] = jnp.exp2(dot(left[at : at + ROWS, :], right[...], NT) * LOG2E).astype(BF16)


def doubled(d):
    return jnp.concatenate([d, d], axis=0)


def forward(d, tile):
    return dot(doubled(d), tile, NN)[: d.shape[0]]


def across(d, tile):
    return dot(doubled(doubled(d)), tile, NT)[: d.shape[0]]


def following(targets, d, w):
    residual = targets - (d + w)
    return residual, KEEP * d + GAIN * residual


def spans(n):
    cuts = [n * sum(SHARES[:j]) // sum(SHARES) for j in range(PIECES + 1)]
    return [(a, b - a) for a, b in zip(cuts, cuts[1:])]


def prep_kernel(size, masks, x, t, whole, *rest):
    parts, branch, case, t_in, flags_in, sems = rest[:PIECES], *rest[PIECES:]
    n = x.shape[0]
    rhs = t.shape[0]
    flags = pltpu.make_async_copy(masks, flags_in, sems.at[2 + PIECES])
    flags.start()
    copies = [pltpu.make_async_copy(t, t_in, sems.at[0])]
    copies.append(pltpu.make_async_copy(x, whole.at[pl.ds(0, n)], sems.at[1]))
    for j, (at, rows) in enumerate(spans(n)):
        copies.append(
            pltpu.make_async_copy(x.at[pl.ds(at, rows)], parts[j].at[pl.ds(0, rows)], sems.at[2 + j])
        )
    for copy in copies:
        copy.start()
    flags.wait()
    first, second = flags_in[0], flags_in[1]
    other = jnp.where(first == size - 1, second, first)
    far = other >= size // 2
    case[0] = jnp.where(far, 1, 0)
    branch[0] = jnp.where(far, size - 1 - other, other) - 1
    copies[0].wait()
    d = (t_in[...] / CENTER).astype(BF16)
    for part, (at, rows) in zip((whole,) + tuple(parts), [(0, n)] + spans(n)):
        for j in range(rows // 128):
            part[rows + rhs * j : rows + rhs * (j + 1), :] = d[:, at + 128 * j : at + 128 * (j + 1)]
    for copy in copies[1:]:
        copy.wait()


def main_kernel(weight, case, x, t, near, *rest):
    far, late = rest[:PIECES], rest[PIECES : 2 * PIECES]
    (sol, res, xs, slabs, t_in, d_all, left, right, kept, once, sol_out, res_out, sems, more) = rest[2 * PIECES :]
    n, feat = x.shape
    rhs = t.shape[0]
    own = [
        pltpu.make_async_copy(x, xs.at[0], more.at[0]),
        pltpu.make_async_copy(t, t_in, more.at[1]),
    ]
    others = []
    for j, (start, rows) in enumerate(spans(n)):
        deep = rows * rhs // feat
        at, low = pl.ds(start, rows), pl.ds(start * rhs // feat, deep)
        for slot in (1, 2, 3):
            if slot == 1:
                sources = near.at[at], near.at[pl.ds(n + start * rhs // feat, deep)]
            else:
                packet = (far, late)[slot - 2][j]
                sources = packet.at[pl.ds(0, rows)], packet.at[pl.ds(rows, deep)]
            others.append(pltpu.make_async_copy(sources[0], xs.at[slot, at], sems.at[slot - 1, j]))
            others.append(pltpu.make_async_copy(sources[1], slabs.at[slot - 1, low], sems.at[slot - 1, PIECES + j]))
    for copy in own + others:
        copy.start()
    e, o = 1 + case[0], 2 - case[0]
    own[0].wait()
    sides(xs[0], left.at[0], right.at[0])
    tile_into(kept.at[0], left.at[0], right.at[0])
    own[1].wait()
    first = t_in[...] / CENTER
    d0 = first.astype(BF16)
    w0 = forward(d0, kept[0])
    for copy in others:
        copy.wait()
    for slot, source in ((1, e), (2, o), (3, 3)):
        for j in range(n // feat):
            d_all[slot - 1, :, feat * j : feat * (j + 1)] = slabs[source - 1, rhs * j : rhs * (j + 1), :]
        sides(xs[source], left.at[slot], None if slot == 2 else right.at[1 if slot == 1 else 2])
    de, do, da = d_all[0], d_all[1], d_all[2]
    tile_into(kept.at[1], left.at[1], right.at[0])
    tile_into(kept.at[2], left.at[3], right.at[0])
    tile_into(once.at[0], left.at[1], right.at[1])
    tile_into(once.at[1], left.at[2], right.at[1])
    tile_into(once.at[2], left.at[3], right.at[2])
    tile_into(once.at[3], left.at[2], right.at[2])
    w0 = w0 + forward(de, kept[1]) + forward(da, kept[2])
    we = across(d0, kept[1]) + forward(de, once[0]) + forward(do, once[1])
    wa = across(d0, kept[2]) + forward(da, once[2]) + forward(do, once[3])
    residual, second = following(t_in[...], first, weight * w0)
    e_first, a_first = de.astype(F32), da.astype(F32)
    _, e_second = following(e_first * CENTER, e_first, weight * we)
    _, a_second = following(a_first * CENTER, a_first, weight * wa)
    sol_out[...] = first + second
    sent = pltpu.make_async_copy(sol_out, sol, more.at[2])
    sent.start()
    w = forward(second.astype(BF16), kept[0])
    w = w + forward(e_second.astype(BF16), kept[1])
    w = w + forward(a_second.astype(BF16), kept[2])
    res_out[...] = residual - (second + weight * w)
    last = pltpu.make_async_copy(res_out, res, more.at[3])
    last.start()
    sent.wait()
    last.wait()


def call(kernel, outs, spaces, scratch, args, scalars, limit):
    hbm = pl.BlockSpec(memory_space=pl.ANY)
    smem = pl.BlockSpec(memory_space=pltpu.SMEM)
    return pl.pallas_call(
        kernel,
        out_shape=outs,
        in_specs=[smem] * scalars + [hbm] * (len(args) - scalars),
        out_specs=[pl.BlockSpec(memory_space=space) for space in spaces],
        scratch_shapes=scratch,
        compiler_params=pltpu.CompilerParams(vmem_limit_bytes=limit),
    )(*args)


def swap(array, mask):
    return lax.ppermute(array, "blk", [(i, i ^ mask) for i in range(lax.axis_size("blk"))])


def relay(array, mask):
    for bit in range(lax.axis_size("blk").bit_length() - 1):
        taken = jnp.bitwise_and(jnp.right_shift(mask, bit), 1) == 1
        array = jnp.where(taken, swap(array, 1 << bit), array)
    return array


def body(points, targets, masks):
    n, feat = points.shape
    rhs = targets.shape[1]
    size = lax.axis_size("blk")
    weight = 384.0 / ((ROUNDS + 1) * n)
    t = targets.T
    length = n + n * rhs // feat
    shape = jax.ShapeDtypeStruct
    dma = pltpu.SemaphoreType.DMA
    whole, *rest = call(
        functools.partial(prep_kernel, size),
        [shape((length, feat), BF16)]
        + [shape((rows * length // n, feat), BF16) for _, rows in spans(n)]
        + [shape((1,), jnp.int32)] * 2,
        [pltpu.VMEM] * (1 + PIECES) + [pltpu.SMEM] * 2,
        [pltpu.VMEM((rhs, n), F32), pltpu.SMEM((ROUNDS,), jnp.int32), dma((3 + PIECES,))],
        (masks, points, t),
        0,
        PREP << 20,
    )
    parts, branch, case = rest[:PIECES], rest[PIECES], rest[PIECES + 1]

    def exchange(mask):
        def run(whole, *parts):
            near = swap(whole, mask)
            first = swap(parts[0], (size - 1) ^ mask)
            direct = swap(parts[1], size - 1)
            first, near = lax.optimization_barrier((first, near))
            passed = swap(first, mask)
            if mask == 1:
                direct, passed = lax.optimization_barrier((direct, passed))
                return near, [first, swap(direct, mask)], [passed, direct]
            second, first = lax.optimization_barrier((parts[1], first))
            return near, [first, swap(second, (size - 1) ^ mask)], [passed, direct]

        return run

    if size <= 32:
        near, far, late = lax.switch(
            branch[0], [exchange(mask) for mask in range(1, size // 2)], whole, *parts
        )
    else:
        mask = branch[0] + 1
        far = [relay(part, (size - 1) ^ mask) for part in parts]
        near, late = relay(whole, mask), [relay(part, mask) for part in far]
    sol, res = call(
        functools.partial(main_kernel, weight),
        [shape((rhs, n), F32)] * 2,
        [pl.ANY] * 2,
        [
            pltpu.VMEM((4, n, feat), BF16),
            pltpu.VMEM((3, n * rhs // feat, feat), BF16),
            pltpu.VMEM((rhs, n), F32),
            pltpu.VMEM((3, rhs, n), BF16),
            pltpu.VMEM((4, n, 2 * feat), BF16),
            pltpu.VMEM((3, n, 2 * feat), BF16),
            pltpu.VMEM((3, n, n), BF16),
            pltpu.VMEM((4, n, n), BF16),
            pltpu.VMEM((rhs, n), F32),
            pltpu.VMEM((rhs, n), F32),
            dma((3, 2 * PIECES)),
            dma((4,)),
        ],
        (case, points, t, near, *far, *late),
        1,
        40 << 20,
    )
    return sol.T, res.T


def solution(mesh):
    placed = (P("blk", None), P("blk", None), P())
    return jax.shard_map(
        body,
        mesh=mesh,
        in_specs=placed,
        out_specs=(P("blk", None), P("blk", None)),
        check_vma=False,
    )
```

```python
import functools

import jax
import jax.numpy as jnp
from jax import lax
from jax.experimental import pallas as pl
from jax.experimental.pallas import tpu as pltpu
from jax.sharding import PartitionSpec as P

ROUNDS = 2
F32 = jnp.float32
BF16 = jnp.bfloat16
LOG2E = 1.4426950408889634
NN = (((1,), (0,)), ((), ()))
NT = (((1,), (1,)), ((), ()))
LOWEST, HIGHEST = 1.0, 25.0
CENTER = (HIGHEST + LOWEST) / 2.0
HALF = (HIGHEST - LOWEST) / 2.0
SIGMA = CENTER / HALF
FIRST = 1.0 / (2.0 * SIGMA - 1.0 / SIGMA)
KEEP = FIRST / SIGMA
GAIN = 2.0 * FIRST / HALF
ROWS = 256
PREP = 56
SHARES = (4, 4)
PIECES = len(SHARES)


def dot(a, b, dims):
    return lax.dot_general(a, b, dims, preferred_element_type=F32)


def sides(x, left_ref, right_ref):
    feat = x.shape[1]
    xf = x.astype(F32)
    norm = jnp.sum(xf * xf, axis=1, keepdims=True) * (-1.0 / feat)
    high = norm.astype(BF16).astype(F32)
    mid = (norm - high).astype(BF16).astype(F32)
    low = norm - high - mid
    lane = lax.broadcasted_iota(jnp.int32, x.shape, 1)

    def extra(norms, ones):
        values = jnp.where((lane >= ones) & (lane < ones + 3), 1.0, 0.0)
        for place, part in enumerate((high, mid, low)):
            values = jnp.where(lane == norms + place, part, values)
        return values.astype(BF16)

    left_ref[:, :feat] = (xf * (2.0 / feat)).astype(BF16)
    left_ref[:, feat:] = extra(0, 3)
    if right_ref is not None:
        right_ref[:, :feat] = x
        right_ref[:, feat:] = extra(3, 0)


def tile_into(out, left, right):
    out[...] = jnp.exp2(dot(left[...], right[...], NT) * LOG2E).astype(BF16)


def symmetric_into(out, left, right):
    n = left.shape[0]
    for at in range(0, n, ROWS):
        part = jnp.exp2(dot(left[at : at + ROWS, :], right[at:, :], NT) * LOG2E).astype(BF16)
        out[at : at + ROWS, at:] = part
        for low in range(at + ROWS, n, ROWS):
            out[low : low + ROWS, at : at + ROWS] = part[:, low - at : low - at + ROWS].T


def doubled(d):
    return jnp.concatenate([d, d], axis=0)


def forward(d, tile):
    return dot(doubled(d), tile, NN)[: d.shape[0]]


def across(d, tile):
    return dot(doubled(doubled(d)), tile, NT)[: d.shape[0]]


def following(targets, d, w):
    residual = targets - (d + w)
    return residual, KEEP * d + GAIN * residual


def spans(n):
    cuts = [n * sum(SHARES[:j]) // sum(SHARES) for j in range(PIECES + 1)]
    return [(a, b - a) for a, b in zip(cuts, cuts[1:])]


def prep_kernel(size, masks, x, t, whole, *rest):
    parts, branch, case, t_in, flags_in, sems = rest[:PIECES], *rest[PIECES:]
    n = x.shape[0]
    rhs = t.shape[0]
    flags = pltpu.make_async_copy(masks, flags_in, sems.at[2 + PIECES])
    flags.start()
    copies = [pltpu.make_async_copy(t, t_in, sems.at[0])]
    copies.append(pltpu.make_async_copy(x, whole.at[pl.ds(0, n)], sems.at[1]))
    for j, (at, rows) in enumerate(spans(n)):
        copies.append(
            pltpu.make_async_copy(x.at[pl.ds(at, rows)], parts[j].at[pl.ds(0, rows)], sems.at[2 + j])
        )
    for copy in copies:
        copy.start()
    flags.wait()
    first, second = flags_in[0], flags_in[1]
    other = jnp.where(first == size - 1, second, first)
    far = other >= size // 2
    case[0] = jnp.where(far, 1, 0)
    branch[0] = jnp.where(far, size - 1 - other, other) - 1
    copies[0].wait()
    d = (t_in[...] / CENTER).astype(BF16)
    for part, (at, rows) in zip((whole,) + tuple(parts), [(0, n)] + spans(n)):
        for j in range(rows // 128):
            part[rows + rhs * j : rows + rhs * (j + 1), :] = d[:, at + 128 * j : at + 128 * (j + 1)]
    for copy in copies[1:]:
        copy.wait()


def main_kernel(weight, case, x, t, near, *rest):
    far, late = rest[:PIECES], rest[PIECES : 2 * PIECES]
    (sol, res, xs, slabs, t_in, d_all, left, right, kept, once, sol_out, res_out, sems, more) = rest[2 * PIECES :]
    n, feat = x.shape
    rhs = t.shape[0]
    own = [
        pltpu.make_async_copy(x, xs.at[0], more.at[0]),
        pltpu.make_async_copy(t, t_in, more.at[1]),
    ]
    others = {slot: [] for slot in (1, 2, 3)}
    for slot, copies in others.items():
        for j, (start, rows) in enumerate(spans(n)):
            deep = rows * rhs // feat
            at, low = pl.ds(start, rows), pl.ds(start * rhs // feat, deep)
            if slot == 1:
                sources = near.at[at], near.at[pl.ds(n + start * rhs // feat, deep)]
            else:
                packet = (far, late)[slot - 2][j]
                sources = packet.at[pl.ds(0, rows)], packet.at[pl.ds(rows, deep)]
            copies.append(pltpu.make_async_copy(sources[0], xs.at[slot, at], sems.at[slot - 1, j]))
            copies.append(pltpu.make_async_copy(sources[1], slabs.at[slot - 1, low], sems.at[slot - 1, PIECES + j]))
    for copy in own + others[1] + others[2] + others[3]:
        copy.start()

    def unpack(slot, source):
        for j in range(n // feat):
            d_all[slot - 1, :, feat * j : feat * (j + 1)] = slabs[source - 1, rhs * j : rhs * (j + 1), :]
        return d_all[slot - 1]

    e, o = 1 + case[0], 2 - case[0]
    own[0].wait()
    sides(xs[0], left.at[0], right.at[0])
    symmetric_into(kept.at[0], left.at[0], right.at[0])
    own[1].wait()
    first = t_in[...] / CENTER
    d0 = first.astype(BF16)
    w0 = forward(d0, kept[0])
    for copy in others[1] + others[2]:
        copy.wait()
    de, do = unpack(1, e), unpack(2, o)
    sides(xs[e], left.at[1], right.at[1])
    sides(xs[o], left.at[2], None)
    tile_into(kept.at[1], left.at[1], right.at[0])
    symmetric_into(once.at[0], left.at[1], right.at[1])
    tile_into(once.at[1], left.at[2], right.at[1])
    w0 = w0 + forward(de, kept[1])
    we = across(d0, kept[1]) + forward(de, once[0]) + forward(do, once[1])
    for copy in others[3]:
        copy.wait()
    da = unpack(3, 3)
    sides(xs[3], left.at[3], right.at[2])
    tile_into(kept.at[2], left.at[3], right.at[0])
    symmetric_into(once.at[2], left.at[3], right.at[2])
    tile_into(once.at[3], left.at[2], right.at[2])
    w0 = w0 + forward(da, kept[2])
    wa = across(d0, kept[2]) + forward(da, once[2]) + forward(do, once[3])
    residual, second = following(t_in[...], first, weight * w0)
    e_first, a_first = de.astype(F32), da.astype(F32)
    _, e_second = following(e_first * CENTER, e_first, weight * we)
    _, a_second = following(a_first * CENTER, a_first, weight * wa)
    sol_out[...] = first + second
    sent = pltpu.make_async_copy(sol_out, sol, more.at[2])
    sent.start()
    w = forward(second.astype(BF16), kept[0])
    w = w + forward(e_second.astype(BF16), kept[1])
    w = w + forward(a_second.astype(BF16), kept[2])
    res_out[...] = residual - (second + weight * w)
    last = pltpu.make_async_copy(res_out, res, more.at[3])
    last.start()
    sent.wait()
    last.wait()


def call(kernel, outs, spaces, scratch, args, scalars, limit):
    hbm = pl.BlockSpec(memory_space=pl.ANY)
    smem = pl.BlockSpec(memory_space=pltpu.SMEM)
    return pl.pallas_call(
        kernel,
        out_shape=outs,
        in_specs=[smem] * scalars + [hbm] * (len(args) - scalars),
        out_specs=[pl.BlockSpec(memory_space=space) for space in spaces],
        scratch_shapes=scratch,
        compiler_params=pltpu.CompilerParams(vmem_limit_bytes=limit),
    )(*args)


def swap(array, mask):
    return lax.ppermute(array, "blk", [(i, i ^ mask) for i in range(lax.axis_size("blk"))])


def relay(array, mask):
    for bit in range(lax.axis_size("blk").bit_length() - 1):
        taken = jnp.bitwise_and(jnp.right_shift(mask, bit), 1) == 1
        array = jnp.where(taken, swap(array, 1 << bit), array)
    return array


def body(points, targets, masks):
    n, feat = points.shape
    rhs = targets.shape[1]
    size = lax.axis_size("blk")
    weight = 384.0 / ((ROUNDS + 1) * n)
    t = targets.T
    length = n + n * rhs // feat
    shape = jax.ShapeDtypeStruct
    dma = pltpu.SemaphoreType.DMA
    whole, *rest = call(
        functools.partial(prep_kernel, size),
        [shape((length, feat), BF16)]
        + [shape((rows * length // n, feat), BF16) for _, rows in spans(n)]
        + [shape((1,), jnp.int32)] * 2,
        [pltpu.VMEM] * (1 + PIECES) + [pltpu.SMEM] * 2,
        [pltpu.VMEM((rhs, n), F32), pltpu.SMEM((ROUNDS,), jnp.int32), dma((3 + PIECES,))],
        (masks, points, t),
        0,
        PREP << 20,
    )
    parts, branch, case = rest[:PIECES], rest[PIECES], rest[PIECES + 1]

    def exchange(mask):
        def run(whole, *parts):
            crossing = (size - 1) ^ mask
            near = swap(whole, mask)
            first = swap(parts[0], crossing)
            direct = swap(parts[1], size - 1)
            early, reached = lax.optimization_barrier((parts[1], first))
            first, near = lax.optimization_barrier((reached, near))
            passed = swap(first, mask)
            if mask == 1:
                direct, passed = lax.optimization_barrier((direct, passed))
                return near, [first, swap(direct, mask)], [passed, direct]
            late, first = lax.optimization_barrier((parts[1], first))
            return near, [first, swap(early if mask >= size // 4 else late, crossing)], [passed, direct]

        return run

    if size <= 32:
        near, far, late = lax.switch(
            branch[0], [exchange(mask) for mask in range(1, size // 2)], whole, *parts
        )
    else:
        mask = branch[0] + 1
        far = [relay(part, (size - 1) ^ mask) for part in parts]
        near, late = relay(whole, mask), [relay(part, mask) for part in far]
    sol, res = call(
        functools.partial(main_kernel, weight),
        [shape((rhs, n), F32)] * 2,
        [pl.ANY] * 2,
        [
            pltpu.VMEM((4, n, feat), BF16),
            pltpu.VMEM((3, n * rhs // feat, feat), BF16),
            pltpu.VMEM((rhs, n), F32),
            pltpu.VMEM((3, rhs, n), BF16),
            pltpu.VMEM((4, n, 2 * feat), BF16),
            pltpu.VMEM((3, n, 2 * feat), BF16),
            pltpu.VMEM((3, n, n), BF16),
            pltpu.VMEM((4, n, n), BF16),
            pltpu.VMEM((rhs, n), F32),
            pltpu.VMEM((rhs, n), F32),
            dma((3, 2 * PIECES)),
            dma((4,)),
        ],
        (case, points, t, near, *far, *late),
        1,
        40 << 20,
    )
    return sol.T, res.T


def solution(mesh):
    placed = (P("blk", None), P("blk", None), P())
    return jax.shard_map(
        body,
        mesh=mesh,
        in_specs=placed,
        out_specs=(P("blk", None), P("blk", None)),
        check_vma=False,
    )
```
